32 devices in a mesh: space: 8 (over y, x, core), orb: 4 (over z).
Axes of the slice: x: 2, y: 2, z: 4, core: 2. Of those that a mesh axis runs over, the one named last changes fastest.
Arguments:
- orbitals: float32 [64, 16, 32, 512], P('space', None, None, 'orb'), may hold values from -75 to 75
- potential: float32 [64, 16, 32], P('space'), may hold values from -2 to 0
Outputs:
- whitened: float32 [64, 16, 32, 512], P('space', None, None, 'orb')
The draws below stay inside these ranges and needn't reach their ends.
All inputs are finite; a program needn't handle non-finite values.
Results may differ from the reference program's by a relative error of at most 0.0003.
Values sent between devices are 32-bit elements; how exact they have to be, the bound alone decides.
A program may use at most 192 MiB of HBM per device.

```python
import math
import jax
import jax.numpy as jnp
from jax import lax

NY = 16
NZ = 32
NORB = 512
DEGREE = 4
NS_ITERS = 8
NX = 64
NCELLS = 32768


def draw_orbitals(key, part):
    key = jax.random.fold_in(key, 11)
    base_key, scale_key = jax.random.split(key, 2)
    base_values = jnp.clip(jax.random.normal(base_key, (NX, NY, NZ, NORB), jnp.float32), -5.0, 5.0)
    mixed = base_values + 0.4 * jnp.roll(base_values, 1, axis=3)
    column_scales = jnp.exp(jax.random.uniform(scale_key, (NORB,), jnp.float32, 0.0, math.log(10.0)))
    return (mixed * column_scales).astype(jnp.float32)


def block_levels(rng, extent, cuts, least, top_value):
    loudness, own = 1.0, jax.random.fold_in(rng, 6)
    for axis_at, parts in cuts:
        heights = jnp.exp(jax.random.uniform(jax.random.fold_in(own, axis_at), (parts,), jnp.float32, least / len(cuts), top_value / len(cuts)))
        loudness = loudness * jnp.repeat(heights, extent[axis_at] // parts).reshape([-1 if axis == axis_at else 1 for axis in range(len(extent))])
    return loudness


def setup_inputs(seed: int = 0) -> dict:
    splits = jax.random.split(jax.random.key(seed), 3)
    return {
        "orbitals": draw_orbitals(jax.random.fold_in(splits[2], 71), 0),
        "potential": jnp.clip(-2.0 + 2.0 * jax.random.uniform(splits[1], (NX, NY, NZ), jnp.float32) ** block_levels(splits[1], (NX, NY, NZ), ((0, 8),), -0.2, 0.2), -2.0, 0.0),
    }


STENCIL_WEIGHTS = [-49.0 / 18.0, 3.0 / 2.0, -3.0 / 20.0, 1.0 / 90.0]
CENTER = 5.0
HALF_WIDTH = 4.0

def apply_hamiltonian(field, potential):
    laplace = 3.0 * STENCIL_WEIGHTS[0] * field
    for offset in range(1, 4):
        for axis_number in range(3):
            laplace = laplace + STENCIL_WEIGHTS[offset] * (jnp.roll(field, offset, axis_number) + jnp.roll(field, -offset, axis_number))
    return -0.5 * laplace + potential[..., None] * field

def whiten_factor(intersection):
    norm_scale = jnp.sqrt(jnp.sum(intersection * intersection) + 1e-06)
    identity = jnp.eye(intersection.shape[0], dtype=jnp.float32)
    scaled = intersection / norm_scale
    inverse = identity
    for step in range(NS_ITERS):
        factor = 1.5 * identity - 0.5 * jnp.dot(inverse, scaled, precision=lax.Precision.HIGHEST)
        scaled = jnp.dot(scaled, factor, precision=lax.Precision.HIGHEST)
        inverse = jnp.dot(factor, inverse, precision=lax.Precision.HIGHEST)
    return inverse / jnp.sqrt(norm_scale)

def reference(orbitals, potential):
    previous = orbitals
    current = (apply_hamiltonian(orbitals, potential) - CENTER * orbitals) / HALF_WIDTH
    for degree_step in range(2, DEGREE + 1):
        following = 2.0 * (apply_hamiltonian(current, potential) - CENTER * current) / HALF_WIDTH - previous
        previous = current
        current = following
    cell_rows = current.reshape(-1, current.shape[-1])
    intersection = jnp.dot(cell_rows.T, cell_rows, precision=lax.Precision.HIGHEST) / NCELLS
    root_inverse = whiten_factor(intersection)
    whitened = jnp.dot(cell_rows, root_inverse, precision=lax.Precision.HIGHEST)
    return whitened.reshape(current.shape)
```

```python
import jax
import jax.numpy as jnp
from jax import lax
from jax.sharding import PartitionSpec as P

DEGREE = 4
NS_ITERS = 8


STENCIL_WEIGHTS = [-49.0 / 18.0, 3.0 / 2.0, -3.0 / 20.0, 1.0 / 90.0]
CENTER = 5.0
HALF_WIDTH = 4.0


def padded_2(cells, sides, width):
    for axis, dim in sides:
        count = lax.axis_size(axis)
        head = lax.slice_in_dim(cells, 0, width, axis=dim)
        tail = lax.slice_in_dim(cells, cells.shape[dim] - width, cells.shape[dim], axis=dim)
        cells = jnp.concatenate(
            [
                lax.ppermute(tail, axis, [(i, (i + 1) % count) for i in range(count)]),
                cells,
                lax.ppermute(head, axis, [((i + 1) % count, i) for i in range(count)]),
            ],
            axis=dim,
        )
    return cells


def slab_hamiltonian(field, potential):
    padded = padded_2(field, (("space", 0),), 3)
    planes = field.shape[0]
    laplace = 3.0 * STENCIL_WEIGHTS[0] * field
    for offset in range(1, 4):
        along_first = (
            padded[3 + offset : 3 + offset + planes] + padded[3 - offset : 3 - offset + planes]
        )
        along_second = jnp.roll(field, offset, 1) + jnp.roll(field, -offset, 1)
        along_third = jnp.roll(field, offset, 2) + jnp.roll(field, -offset, 2)
        laplace = laplace + STENCIL_WEIGHTS[offset] * (along_first + along_second + along_third)
    return -0.5 * laplace + potential[..., None] * field


def chebyshev(start, apply_operator):
    previous = start
    current = (apply_operator(start) - CENTER * start) / HALF_WIDTH
    for degree_step in range(2, DEGREE + 1):
        following = 2.0 * (apply_operator(current) - CENTER * current) / HALF_WIDTH - previous
        previous = current
        current = following
    return current


def product(left, right):
    return jnp.dot(left, right, precision=lax.Precision.HIGH)


def whiten_factor(intersection):
    norm_scale = jnp.sqrt(jnp.sum(intersection * intersection) + 1e-06)
    identity = jnp.eye(intersection.shape[0], dtype=jnp.float32)
    scaled = intersection / norm_scale
    inverse = 1.5 * identity - 0.5 * scaled
    scaled = product(scaled, inverse)
    for step in range(1, NS_ITERS):
        factor = 1.5 * identity - 0.5 * product(inverse, scaled)
        if step < NS_ITERS - 1:
            scaled = product(scaled, factor)
        inverse = product(factor, inverse)
    return inverse / jnp.sqrt(norm_scale)


def body(orbitals, potential):
    local_orbs = orbitals.shape[-1]

    def slab_operator(field):
        return slab_hamiltonian(field, potential)

    filtered = chebyshev(orbitals, slab_operator)
    cell_rows = filtered.reshape(-1, local_orbs)
    total_cells = cell_rows.shape[0] * lax.axis_size("space")
    mixed = lax.all_to_all(cell_rows, "orb", split_axis=0, concat_axis=1, tiled=True)
    partial_terms = product(mixed.T, mixed)
    intersection = lax.psum(partial_terms, ("space", "orb")) / total_cells
    whitened = product(mixed, whiten_factor(intersection))
    whitened = lax.all_to_all(whitened, "orb", split_axis=1, concat_axis=0, tiled=True)
    return whitened.reshape(filtered.shape)


def solution(mesh):
    return jax.shard_map(
        body,
        mesh=mesh,
        in_specs=(P("space", None, None, "orb"), P("space", None, None)),
        out_specs=P("space", None, None, "orb"),
        check_vma=False,
    )
```

```python
import functools

import jax
import jax.numpy as jnp
from jax import lax
from jax.experimental import pallas as pl
from jax.experimental.pallas import tpu as pltpu
from jax.sharding import PartitionSpec as P

DEGREE = 4
NS_ITERS = 8

STENCIL_WEIGHTS = [-49.0 / 18.0, 3.0 / 2.0, -3.0 / 20.0, 1.0 / 90.0]
CENTER = 5.0
HALF_WIDTH = 4.0
REACH = 3
CHUNKS = 4
MESH = pl.DeviceIdType.MESH


def split(value):
    high = value.astype(jnp.bfloat16)
    low = (value - high.astype(jnp.float32)).astype(jnp.bfloat16)
    return high, low


def product(left, right):
    def dot(a, b):
        return jnp.dot(a, b, preferred_element_type=jnp.float32)

    return dot(left[0], right[0]) + (dot(left[0], right[1]) + dot(left[1], right[0]))


def transposed_dot(left, right):
    return lax.dot_general(
        left, right, (((0,), (0,)), ((), ())), preferred_element_type=jnp.float32
    )


def kernel(
    n_space, n_orb, x_ref, coef_ref, out_ref,
    fields, last, mixed, high, low, part, cross, landed, summed, landed_cols, total, y_ref, z_ref, white,
    load_sem, halo_send, halo_recv, to_send, to_recv, to_own,
    rows_send, rows_recv, cols_send, cols_recv, gcols_send, gcols_recv, grows_send, grows_recv,
    back_send, back_recv, back_own,
):
    planes, ny, nz, lanes = x_ref.shape
    norb = total.shape[0]
    rows = ny // CHUNKS
    share = planes // n_orb
    cells = share * rows * nz
    piece = norb // n_space
    me_s = lax.axis_index("space")
    me_o = lax.axis_index("orb")
    left = lax.rem(me_s + n_space - 1, n_space)
    right = lax.rem(me_s + 1, n_space)

    def space_peer(offset):
        return lax.rem(me_s + offset, n_space)

    def orb_peer(offset):
        return lax.rem(me_o + offset, n_orb)

    def row_block(device):
        return pl.ds(pl.multiple_of(device * piece, piece), piece)

    def lane_block(device):
        return pl.ds(pl.multiple_of(device * lanes, lanes), lanes)

    def remote(src, dst, send, recv, space, orb):
        return pltpu.make_async_remote_copy(
            src_ref=src, dst_ref=dst, send_sem=send, recv_sem=recv,
            device_id=(space, orb), device_id_type=MESH,
        )

    load = pltpu.make_async_copy(x_ref, fields.at[0, pl.ds(REACH, planes)], load_sem)
    load.start()

    barrier = pltpu.get_barrier_semaphore()
    for offset in range(1, n_space):
        pl.semaphore_signal(barrier, inc=1, device_id=(space_peer(offset), me_o), device_id_type=MESH)
    for offset in range(1, n_orb):
        pl.semaphore_signal(barrier, inc=1, device_id=(me_s, orb_peer(offset)), device_id_type=MESH)
    pl.semaphore_wait(barrier, n_space + n_orb - 2)

    def halo(step, chunk, side):
        start, landing = ((REACH, REACH + planes), (planes, 0))[side]
        ys = pl.ds(chunk * rows, rows)
        return remote(
            fields.at[step, pl.ds(start, REACH), ys],
            fields.at[step, pl.ds(landing, REACH), ys],
            halo_send.at[step, chunk, side],
            halo_recv.at[step, chunk, side],
            (left, right)[side],
            me_o,
        )

    def outward(chunk, offset):
        peer = orb_peer(offset)
        return remote(
            last.at[pl.ds(peer * share, share), pl.ds(chunk * rows, rows)],
            mixed.at[chunk, :, :, :, lane_block(me_o)],
            to_send.at[chunk, offset],
            to_recv.at[chunk, offset],
            me_s,
            peer,
        )

    def outward_own(chunk):
        return pltpu.make_async_copy(
            last.at[pl.ds(me_o * share, share), pl.ds(chunk * rows, rows)],
            mixed.at[chunk, :, :, :, lane_block(me_o)],
            to_own.at[chunk],
        )

    def back(chunk, offset):
        peer = orb_peer(offset)
        return remote(
            white.at[chunk, :, :, :, lane_block(peer)],
            out_ref.at[pl.ds(me_o * share, share), pl.ds(chunk * rows, rows)],
            back_send.at[chunk, offset],
            back_recv.at[chunk, offset],
            me_s,
            peer,
        )

    def back_own_copy(chunk):
        return pltpu.make_async_copy(
            white.at[chunk, :, :, :, lane_block(me_o)],
            out_ref.at[pl.ds(me_o * share, share), pl.ds(chunk * rows, rows)],
            back_own.at[chunk],
        )

    load.wait()

    @pl.loop(0, CHUNKS)
    def _(chunk):
        halo(0, chunk, 0).start()
        halo(0, chunk, 1).start()

    for step in range(DEGREE):
        scale = (1.0 if step == 0 else 2.0) / HALF_WIDTH
        weights = [-0.5 * scale * w for w in STENCIL_WEIGHTS]

        @pl.loop(0, CHUNKS)
        def _(chunk):
            halo(step, chunk, 0).wait_recv()
            halo(step, chunk, 1).wait_recv()

            @pl.loop(0, planes)
            def _(plane):
                for row in range(rows):
                    y = chunk * rows + row
                    here = fields[step, plane + REACH, y]
                    value = (scale * coef_ref[plane, y]) * here
                    for k in range(1, REACH + 1):
                        along = (
                            fields[step, plane + (REACH + k), y] + fields[step, plane + (REACH - k), y]
                        ) + (
                            fields[step, plane + REACH, lax.rem(y + k, ny)]
                            + fields[step, plane + REACH, lax.rem(y + (ny - k), ny)]
                        )
                        along = along + (pltpu.roll(here, k, 0) + pltpu.roll(here, nz - k, 0))
                        value = value + weights[k] * along
                    if step > 0:
                        value = value - fields[step - 1, plane + REACH, y]
                    if step < DEGREE - 1:
                        fields[step + 1, plane + REACH, y] = value
                    else:
                        last[plane, y] = value

            if step < DEGREE - 1:
                halo(step + 1, chunk, 0).start()
                halo(step + 1, chunk, 1).start()
            else:
                for offset in range(1, n_orb):
                    outward(chunk, offset).start()
                outward_own(chunk).start()

    part[...] = jnp.zeros_like(part)
    cross[...] = jnp.zeros_like(cross)

    @pl.loop(0, CHUNKS)
    def _(chunk):
        for offset in range(1, n_orb):
            outward(chunk, offset).wait_recv()
        outward_own(chunk).wait()
        head, tail = split(mixed[chunk].reshape(cells, norb))
        at = pl.ds(pl.multiple_of(chunk * cells, cells), cells)
        high[at] = head
        low[at] = tail
        part[...] += transposed_dot(head, head)
        cross[...] += transposed_dot(head, tail)

    part[...] = (part[...] + 2.0 * cross[...]) * (1.0 / (CHUNKS * cells * n_space * n_orb))

    def send_rows(offset):
        peer = space_peer(offset)
        return remote(
            part.at[row_block(peer)], landed.at[offset - 1],
            rows_send.at[offset], rows_recv.at[offset], peer, me_o,
        )

    def send_cols(offset):
        peer = orb_peer(offset)
        return remote(
            summed.at[:, lane_block(peer)], landed_cols.at[offset - 1],
            cols_send.at[offset], cols_recv.at[offset], me_s, peer,
        )

    def gather_cols(offset):
        block = total.at[row_block(me_s), lane_block(me_o)]
        return remote(block, block, gcols_send.at[offset], gcols_recv.at[offset], me_s, orb_peer(offset))

    def gather_rows(offset):
        block = total.at[row_block(me_s)]
        return remote(block, block, grows_send.at[offset], grows_recv.at[offset], space_peer(offset), me_o)

    for offset in range(1, n_space):
        send_rows(offset).start()
    value = part[row_block(me_s)]
    for offset in range(1, n_space):
        send_rows(offset).wait_recv()
        value = value + landed[offset - 1]
    summed[...] = value
    for offset in range(1, n_orb):
        send_cols(offset).start()
    value = summed[:, lane_block(me_o)]
    for offset in range(1, n_orb):
        send_cols(offset).wait_recv()
        value = value + landed_cols[offset - 1]
    total[row_block(me_s), lane_block(me_o)] = value
    for offset in range(1, n_orb):
        gather_cols(offset).start()
    for offset in range(1, n_orb):
        gather_cols(offset).wait_recv()
    for offset in range(1, n_space):
        gather_rows(offset).start()
    for offset in range(1, n_space):
        gather_rows(offset).wait_recv()

    one_sided = total[...]
    intersection = 0.5 * (one_sided + one_sided.T)
    squares = jnp.sum(intersection * intersection, axis=0, keepdims=True)
    norm_scale = jnp.sqrt(jnp.sum(squares, axis=1, keepdims=True) + 1e-06)
    on_diagonal = lax.broadcasted_iota(jnp.int32, (norb, norb), 0) == lax.broadcasted_iota(
        jnp.int32, (norb, norb), 1
    )

    def factor_of(term):
        return jnp.where(on_diagonal, 1.5, 0.0) - 0.5 * term

    scaled = intersection / norm_scale
    inverse = factor_of(scaled)
    z_ref[...] = inverse
    y_ref[...] = product(split(scaled), split(inverse))

    @pl.loop(1, NS_ITERS - 1)
    def _(step):
        ys, zs = split(y_ref[...]), split(z_ref[...])
        fs = split(factor_of(product(zs, ys)))
        y_ref[...] = product(ys, fs)
        z_ref[...] = product(fs, zs)

    ys, zs = split(y_ref[...]), split(z_ref[...])
    fs = split(factor_of(product(zs, ys)))
    z_ref[...] = product(fs, zs) / jnp.sqrt(norm_scale)

    @pl.loop(0, CHUNKS)
    def _(chunk):
        at = pl.ds(pl.multiple_of(chunk * cells, cells), cells)
        value = product((high[at], low[at]), split(z_ref[...]))
        white[chunk] = value.reshape(share, rows, nz, norb)
        for offset in range(1, n_orb):
            back(chunk, offset).start()
        back_own_copy(chunk).start()

    for offset in range(1, n_space):
        send_rows(offset).wait_send()
        gather_rows(offset).wait_send()
    for offset in range(1, n_orb):
        send_cols(offset).wait_send()
        gather_cols(offset).wait_send()
    for step in range(DEGREE):

        @pl.loop(0, CHUNKS)
        def _(chunk):
            halo(step, chunk, 0).wait_send()
            halo(step, chunk, 1).wait_send()

    @pl.loop(0, CHUNKS)
    def _(chunk):
        back_own_copy(chunk).wait()
        for offset in range(1, n_orb):
            outward(chunk, offset).wait_send()
            back(chunk, offset).wait()


def body(n_space, n_orb, orbitals, potential):
    planes, ny, nz, lanes = orbitals.shape
    norb = lanes * n_orb
    piece = norb // n_space
    block = (CHUNKS, planes // n_orb, ny // CHUNKS, nz, norb)
    cells = planes * ny * nz // n_orb
    coef = potential - (CENTER + 1.5 * STENCIL_WEIGHTS[0])
    coef = jnp.broadcast_to(coef[..., None], orbitals.shape)
    f32 = jnp.float32
    dma = pltpu.SemaphoreType.DMA
    return pl.pallas_call(
        functools.partial(kernel, n_space, n_orb),
        out_shape=jax.ShapeDtypeStruct(orbitals.shape, f32),
        in_specs=[pl.BlockSpec(memory_space=pl.ANY), pl.BlockSpec(memory_space=pltpu.VMEM)],
        out_specs=pl.BlockSpec(memory_space=pltpu.VMEM),
        scratch_shapes=[
            pltpu.VMEM((DEGREE, planes + 2 * REACH, ny, nz, lanes), f32),
            pltpu.VMEM((planes, ny, nz, lanes), f32),
            pltpu.VMEM(block, f32),
            pltpu.VMEM((cells, norb), jnp.bfloat16),
            pltpu.VMEM((cells, norb), jnp.bfloat16),
            pltpu.VMEM((norb, norb), f32),
            pltpu.VMEM((norb, norb), f32),
            pltpu.VMEM((n_space - 1, piece, norb), f32),
            pltpu.VMEM((piece, norb), f32),
            pltpu.VMEM((n_orb - 1, piece, lanes), f32),
            pltpu.VMEM((norb, norb), f32),
            pltpu.VMEM((norb, norb), f32),
            pltpu.VMEM((norb, norb), f32),
            pltpu.VMEM(block, f32),
            dma,
            dma((DEGREE, CHUNKS, 2)),
            dma((DEGREE, CHUNKS, 2)),
            dma((CHUNKS, n_orb)),
            dma((CHUNKS, n_orb)),
            dma((CHUNKS,)),
            dma((n_space,)),
            dma((n_space,)),
            dma((n_orb,)),
            dma((n_orb,)),
            dma((n_orb,)),
            dma((n_orb,)),
            dma((n_space,)),
            dma((n_space,)),
            dma((CHUNKS, n_orb)),
            dma((CHUNKS, n_orb)),
            dma((CHUNKS,)),
        ],
        compiler_params=pltpu.CompilerParams(
            collective_id=0, has_side_effects=True, vmem_limit_bytes=60 * 1024 * 1024
        ),
        cost_estimate=pl.CostEstimate(
            flops=20_000_000_000, bytes_accessed=8_000_000, transcendentals=0
        ),
    )(orbitals, coef)


def solution(mesh):
    return jax.shard_map(
        functools.partial(body, mesh.shape["space"], mesh.shape["orb"]),
        mesh=mesh,
        in_specs=(P("space", None, None, "orb"), P("space", None, None)),
        out_specs=P("space", None, None, "orb"),
        check_vma=False,
    )
```

```python
import functools

import jax
import jax.numpy as jnp
from jax import lax
from jax.experimental import pallas as pl
from jax.experimental.pallas import tpu as pltpu
from jax.sharding import PartitionSpec as P

DEGREE = 4
NS_ITERS = 8

STENCIL_WEIGHTS = [-49.0 / 18.0, 3.0 / 2.0, -3.0 / 20.0, 1.0 / 90.0]
CENTER = 5.0
HALF_WIDTH = 4.0
REACH = 3
CHUNKS = 4
MESH = pl.DeviceIdType.MESH


def split(value):
    high = value.astype(jnp.bfloat16)
    low = (value - high.astype(jnp.float32)).astype(jnp.bfloat16)
    return high, low


def product(left, right):
    def dot(a, b):
        return jnp.dot(a, b, preferred_element_type=jnp.float32)

    return dot(left[0], right[0]) + (dot(left[0], right[1]) + dot(left[1], right[0]))


def transposed_dot(left, right):
    return lax.dot_general(
        left, right, (((0,), (0,)), ((), ())), preferred_element_type=jnp.float32
    )


def kernel(
    n_space, n_orb, x_ref, coef_ref, out_ref,
    raw, fields, last, mixed, high, low, part, cross, landed, summed, landed_cols, total, y_ref, z_ref, white,
    load_sem, halo_send, halo_recv, to_send, to_recv, to_own,
    rows_send, rows_recv, cols_send, cols_recv, gcols_send, gcols_recv, grows_send, grows_recv,
    back_send, back_recv, back_own,
):
    planes, ny, nz, lanes = x_ref.shape
    norb = total.shape[0]
    rows = ny // CHUNKS
    share = planes // n_orb
    cells = share * rows * nz
    deep = nz // 2
    turn = lanes // 2
    piece = norb // n_space
    me_s = lax.axis_index("space")
    me_o = lax.axis_index("orb")
    left = lax.rem(me_s + n_space - 1, n_space)
    right = lax.rem(me_s + 1, n_space)

    def space_peer(offset):
        return lax.rem(me_s + offset, n_space)

    def orb_peer(offset):
        return lax.rem(me_o + offset, n_orb)

    def row_block(device):
        return pl.ds(pl.multiple_of(device * piece, piece), piece)

    def lane_block(device):
        return pl.ds(pl.multiple_of(device * lanes, lanes), lanes)

    def remote(src, dst, send, recv, space, orb):
        return pltpu.make_async_remote_copy(
            src_ref=src, dst_ref=dst, send_sem=send, recv_sem=recv,
            device_id=(space, orb), device_id_type=MESH,
        )

    load = pltpu.make_async_copy(x_ref, raw, load_sem)
    load.start()

    barrier = pltpu.get_barrier_semaphore()
    for offset in range(1, n_space):
        pl.semaphore_signal(barrier, inc=1, device_id=(space_peer(offset), me_o), device_id_type=MESH)
    for offset in range(1, n_orb):
        pl.semaphore_signal(barrier, inc=1, device_id=(me_s, orb_peer(offset)), device_id_type=MESH)
    pl.semaphore_wait(barrier, n_space + n_orb - 2)

    def halo(half, step, chunk, side):
        start, landing = ((REACH, REACH + planes), (planes, 0))[side]
        ys = pl.ds(chunk * rows, rows)
        return remote(
            fields.at[half, step, pl.ds(start, REACH), ys],
            fields.at[half, step, pl.ds(landing, REACH), ys],
            halo_send.at[half, step, chunk, side],
            halo_recv.at[half, step, chunk, side],
            (left, right)[side],
            me_o,
        )

    def outward(half, chunk, offset):
        peer = orb_peer(offset)
        return remote(
            last.at[half, pl.ds(peer * share, share), pl.ds(chunk * rows, rows)],
            mixed.at[half, chunk, :, :, :, lane_block(me_o)],
            to_send.at[half, chunk, offset],
            to_recv.at[half, chunk, offset],
            me_s,
            peer,
        )

    def outward_own(half, chunk):
        return pltpu.make_async_copy(
            last.at[half, pl.ds(me_o * share, share), pl.ds(chunk * rows, rows)],
            mixed.at[half, chunk, :, :, :, lane_block(me_o)],
            to_own.at[half, chunk],
        )

    def back(chunk, offset):
        peer = orb_peer(offset)
        return remote(
            white.at[chunk, :, :, :, lane_block(peer)],
            out_ref.at[pl.ds(me_o * share, share), pl.ds(chunk * rows, rows)],
            back_send.at[chunk, offset],
            back_recv.at[chunk, offset],
            me_s,
            peer,
        )

    def back_own_copy(chunk):
        return pltpu.make_async_copy(
            white.at[chunk, :, :, :, lane_block(me_o)],
            out_ref.at[pl.ds(me_o * share, share), pl.ds(chunk * rows, rows)],
            back_own.at[chunk],
        )

    load.wait()
    first_lanes = lax.broadcasted_iota(jnp.int32, (deep, lanes), 1) < turn
    sublane = lax.broadcasted_iota(jnp.int32, (8, lanes), 0)

    def turned(value):
        return pltpu.roll(value, turn, value.ndim - 1)

    @pl.loop(0, planes)
    def _(plane):
        @pl.loop(0, ny)
        def _(y):
            top, bottom = raw[plane, y, :deep], raw[plane, y, deep:]
            fields[0, 0, plane + REACH, y] = jnp.where(first_lanes, top, turned(bottom))
            fields[1, 0, plane + REACH, y] = jnp.where(first_lanes, turned(top), bottom)

    def send_halos(half, step):
        @pl.loop(0, CHUNKS)
        def _(chunk):
            halo(half, step, chunk, 0).start()
            halo(half, step, chunk, 1).start()

    def along_depth(here):
        other = turned(here)
        inner = [here[i : i + 8] for i in range(0, deep, 8)]
        groups = [other[deep - 8 :]] + inner + [other[:8]]
        sums = []
        for k in range(1, REACH + 1):
            up = [pltpu.roll(group, k, 0) for group in groups[:-1]]
            down = [pltpu.roll(group, 8 - k, 0) for group in groups[1:]]
            sums.append(
                jnp.concatenate(
                    [
                        jnp.where(sublane < k, up[i], up[i + 1])
                        + jnp.where(sublane >= 8 - k, down[i + 1], down[i])
                        for i in range(len(inner))
                    ],
                    axis=0,
                )
            )
        return sums

    def filter_step(half, step):
        scale = (1.0 if step == 0 else 2.0) / HALF_WIDTH
        weights = [-0.5 * scale * w for w in STENCIL_WEIGHTS]

        @pl.loop(0, CHUNKS)
        def _(chunk):
            halo(half, step, chunk, 0).wait_recv()
            halo(half, step, chunk, 1).wait_recv()

            @pl.loop(0, planes)
            def _(plane):
                at = plane + REACH
                for row in range(rows):
                    y = chunk * rows + row
                    here = fields[half, step, at, y]
                    value = (scale * coef_ref[plane, y]) * here
                    depth = along_depth(here)
                    for k in range(1, REACH + 1):
                        along = (fields[half, step, at + k, y] + fields[half, step, at - k, y]) + (
                            fields[half, step, at, lax.rem(y + k, ny)]
                            + fields[half, step, at, lax.rem(y + (ny - k), ny)]
                        )
                        value = value + weights[k] * (along + depth[k - 1])
                    if step > 0:
                        value = value - fields[half, step - 1, at, y]
                    if step < DEGREE - 1:
                        fields[half, step + 1, at, y] = value
                    else:
                        last[half, plane, y] = value

            if step < DEGREE - 1:
                halo(half, step + 1, chunk, 0).start()
                halo(half, step + 1, chunk, 1).start()
            else:
                for offset in range(1, n_orb):
                    outward(half, chunk, offset).start()
                outward_own(half, chunk).start()

    send_halos(0, 0)
    for step in range(DEGREE - 2):
        filter_step(0, step)
    send_halos(1, 0)
    filter_step(0, DEGREE - 2)
    filter_step(1, 0)
    filter_step(0, DEGREE - 1)
    for step in range(1, DEGREE):
        filter_step(1, step)

    part[...] = jnp.zeros_like(part)
    cross[...] = jnp.zeros_like(cross)

    @pl.loop(0, CHUNKS)
    def _(chunk):
        at = pl.ds(pl.multiple_of(chunk * cells, cells), cells)
        for half in range(2):
            for offset in range(1, n_orb):
                outward(half, chunk, offset).wait_recv()
            outward_own(half, chunk).wait()
        for block in range(n_orb):
            columns = pl.ds(block * lanes, lanes)
            shape = (share * rows, deep, lanes)
            one = mixed[0, chunk, :, :, :, columns].reshape(shape)
            two = mixed[1, chunk, :, :, :, columns].reshape(shape)
            lower = lax.broadcasted_iota(jnp.int32, shape, 2) < turn
            whole = jnp.concatenate(
                [jnp.where(lower, one, turned(two)), jnp.where(lower, turned(one), two)], axis=1
            )
            high[at, columns], low[at, columns] = split(whole.reshape(cells, lanes))
        head, tail = high[at], low[at]
        part[...] += transposed_dot(head, head)
        cross[...] += transposed_dot(head, tail)

    part[...] = (part[...] + 2.0 * cross[...]) * (1.0 / (CHUNKS * cells * n_space * n_orb))

    def send_rows(offset):
        peer = space_peer(offset)
        return remote(
            part.at[row_block(peer)], landed.at[offset - 1],
            rows_send.at[offset], rows_recv.at[offset], peer, me_o,
        )

    def send_cols(offset):
        peer = orb_peer(offset)
        return remote(
            summed.at[:, lane_block(peer)], landed_cols.at[offset - 1],
            cols_send.at[offset], cols_recv.at[offset], me_s, peer,
        )

    def gather_cols(offset):
        block = total.at[row_block(me_s), lane_block(me_o)]
        return remote(block, block, gcols_send.at[offset], gcols_recv.at[offset], me_s, orb_peer(offset))

    def gather_rows(offset):
        block = total.at[row_block(me_s)]
        return remote(block, block, grows_send.at[offset], grows_recv.at[offset], space_peer(offset), me_o)

    for offset in range(1, n_space):
        send_rows(offset).start()
    value = part[row_block(me_s)]
    for offset in range(1, n_space):
        send_rows(offset).wait_recv()
        value = value + landed[offset - 1]
    summed[...] = value
    for offset in range(1, n_orb):
        send_cols(offset).start()
    value = summed[:, lane_block(me_o)]
    for offset in range(1, n_orb):
        send_cols(offset).wait_recv()
        value = value + landed_cols[offset - 1]
    total[row_block(me_s), lane_block(me_o)] = value
    for offset in range(1, n_orb):
        gather_cols(offset).start()
    for offset in range(1, n_orb):
        gather_cols(offset).wait_recv()
    for offset in range(1, n_space):
        gather_rows(offset).start()
    for offset in range(1, n_space):
        gather_rows(offset).wait_recv()

    one_sided = total[...]
    intersection = 0.5 * (one_sided + one_sided.T)
    squares = jnp.sum(intersection * intersection, axis=0, keepdims=True)
    norm_scale = jnp.sqrt(jnp.sum(squares, axis=1, keepdims=True) + 1e-06)
    on_diagonal = lax.broadcasted_iota(jnp.int32, (norb, norb), 0) == lax.broadcasted_iota(
        jnp.int32, (norb, norb), 1
    )

    def factor_of(term):
        return jnp.where(on_diagonal, 1.5, 0.0) - 0.5 * term

    scaled = intersection / norm_scale
    inverse = factor_of(scaled)
    z_ref[...] = inverse
    y_ref[...] = product(split(scaled), split(inverse))

    @pl.loop(1, NS_ITERS - 1)
    def _(step):
        ys, zs = split(y_ref[...]), split(z_ref[...])
        fs = split(factor_of(product(zs, ys)))
        y_ref[...] = product(ys, fs)
        z_ref[...] = product(fs, zs)

    ys, zs = split(y_ref[...]), split(z_ref[...])
    fs = split(factor_of(product(zs, ys)))
    z_ref[...] = product(fs, zs) / jnp.sqrt(norm_scale)

    @pl.loop(0, CHUNKS)
    def _(chunk):
        at = pl.ds(pl.multiple_of(chunk * cells, cells), cells)
        value = product((high[at], low[at]), split(z_ref[...]))
        white[chunk] = value.reshape(share, rows, nz, norb)
        for offset in range(1, n_orb):
            back(chunk, offset).start()
        back_own_copy(chunk).start()

    for offset in range(1, n_space):
        send_rows(offset).wait_send()
        gather_rows(offset).wait_send()
    for offset in range(1, n_orb):
        send_cols(offset).wait_send()
        gather_cols(offset).wait_send()
    for half in range(2):
        for step in range(DEGREE):

            @pl.loop(0, CHUNKS)
            def _(chunk):
                halo(half, step, chunk, 0).wait_send()
                halo(half, step, chunk, 1).wait_send()

    @pl.loop(0, CHUNKS)
    def _(chunk):
        back_own_copy(chunk).wait()
        for offset in range(1, n_orb):
            outward(0, chunk, offset).wait_send()
            outward(1, chunk, offset).wait_send()
            back(chunk, offset).wait()


def body(n_space, n_orb, orbitals, potential):
    planes, ny, nz, lanes = orbitals.shape
    norb = lanes * n_orb
    piece = norb // n_space
    block = (CHUNKS, planes // n_orb, ny // CHUNKS, nz, norb)
    cells = planes * ny * nz // n_orb
    coef = potential - (CENTER + 1.5 * STENCIL_WEIGHTS[0])
    coef = jnp.swapaxes(coef.reshape(planes, ny, 2, nz // 2), 2, 3)
    coef = jnp.broadcast_to(coef[..., None], coef.shape + (lanes // 2,))
    coef = coef.reshape(planes, ny, nz // 2, lanes)
    f32 = jnp.float32
    dma = pltpu.SemaphoreType.DMA
    return pl.pallas_call(
        functools.partial(kernel, n_space, n_orb),
        out_shape=jax.ShapeDtypeStruct(orbitals.shape, f32),
        in_specs=[pl.BlockSpec(memory_space=pl.ANY), pl.BlockSpec(memory_space=pltpu.VMEM)],
        out_specs=pl.BlockSpec(memory_space=pltpu.VMEM),
        scratch_shapes=[
            pltpu.VMEM((planes, ny, nz, lanes), f32),
            pltpu.VMEM((2, DEGREE, planes + 2 * REACH, ny, nz // 2, lanes), f32),
            pltpu.VMEM((2, planes, ny, nz // 2, lanes), f32),
            pltpu.VMEM((2,) + block[:3] + (nz // 2, norb), f32),
            pltpu.VMEM((cells, norb), jnp.bfloat16),
            pltpu.VMEM((cells, norb), jnp.bfloat16),
            pltpu.VMEM((norb, norb), f32),
            pltpu.VMEM((norb, norb), f32),
            pltpu.VMEM((n_space - 1, piece, norb), f32),
            pltpu.VMEM((piece, norb), f32),
            pltpu.VMEM((n_orb - 1, piece, lanes), f32),
            pltpu.VMEM((norb, norb), f32),
            pltpu.VMEM((norb, norb), f32),
            pltpu.VMEM((norb, norb), f32),
            pltpu.VMEM(block, f32),
            dma,
            dma((2, DEGREE, CHUNKS, 2)),
            dma((2, DEGREE, CHUNKS, 2)),
            dma((2, CHUNKS, n_orb)),
            dma((2, CHUNKS, n_orb)),
            dma((2, CHUNKS)),
            dma((n_space,)),
            dma((n_space,)),
            dma((n_orb,)),
            dma((n_orb,)),
            dma((n_orb,)),
            dma((n_orb,)),
            dma((n_space,)),
            dma((n_space,)),
            dma((CHUNKS, n_orb)),
            dma((CHUNKS, n_orb)),
            dma((CHUNKS,)),
        ],
        compiler_params=pltpu.CompilerParams(
            collective_id=0, has_side_effects=True, vmem_limit_bytes=60 * 1024 * 1024
        ),
        cost_estimate=pl.CostEstimate(
            flops=20_000_000_000, bytes_accessed=8_000_000, transcendentals=0
        ),
    )(orbitals, coef)


def solution(mesh):
    return jax.shard_map(
        functools.partial(body, mesh.shape["space"], mesh.shape["orb"]),
        mesh=mesh,
        in_specs=(P("space", None, None, "orb"), P("space", None, None)),
        out_specs=P("space", None, None, "orb"),
        check_vma=False,
    )
```

```python
import functools

import jax
import jax.numpy as jnp
from jax import lax
from jax.experimental import pallas as pl
from jax.experimental.pallas import tpu as pltpu
from jax.sharding import PartitionSpec as P

DEGREE = 4
NS_ITERS = 8

STENCIL_WEIGHTS = [-49.0 / 18.0, 3.0 / 2.0, -3.0 / 20.0, 1.0 / 90.0]
CENTER = 5.0
HALF_WIDTH = 4.0
REACH = 3
CHUNKS = 4
GATHERED = 2
MESH = pl.DeviceIdType.MESH


def split(value):
    high = value.astype(jnp.bfloat16)
    low = (value - high.astype(jnp.float32)).astype(jnp.bfloat16)
    return high, low


def product(left, right):
    return jnp.dot(
        jnp.concatenate([left[0], left[0], left[1]], axis=1),
        jnp.concatenate([right[0], right[1], right[0]], axis=0),
        preferred_element_type=jnp.float32,
    )


def transposed_dot(left, right):
    return lax.dot_general(
        left, right, (((0,), (0,)), ((), ())), preferred_element_type=jnp.float32
    )


def kernel(
    n_space, n_orb, x_ref, potential_ref, out_ref,
    raw, coef_ref, fields, last, mixed, extra, high, low, part, cross, landed, summed, landed_cols, total, y_ref, z_ref, white,
    load_sem, halo_send, halo_recv, to_send, to_recv, to_own, extra_send, extra_recv,
    rows_send, rows_recv, cols_send, cols_recv, gcols_send, gcols_recv, grows_send, grows_recv,
    back_send, back_recv, back_own,
):
    planes, ny, nz, lanes = x_ref.shape
    norb = total.shape[0]
    rows = ny // CHUNKS
    share = planes // n_orb
    cells = share * rows * nz
    deep = nz // 2
    turn = lanes // 2
    piece = norb // n_space
    me_s = lax.axis_index("space")
    me_o = lax.axis_index("orb")
    left = lax.rem(me_s + n_space - 1, n_space)
    right = lax.rem(me_s + 1, n_space)

    def space_peer(offset):
        return lax.rem(me_s + offset, n_space)

    def orb_peer(offset):
        return lax.rem(me_o + offset, n_orb)

    def row_block(device):
        return pl.ds(pl.multiple_of(device * piece, piece), piece)

    def lane_block(device):
        return pl.ds(pl.multiple_of(device * lanes, lanes), lanes)

    def remote(src, dst, send, recv, space, orb):
        return pltpu.make_async_remote_copy(
            src_ref=src, dst_ref=dst, send_sem=send, recv_sem=recv,
            device_id=(space, orb), device_id_type=MESH,
        )

    load = pltpu.make_async_copy(x_ref, raw, load_sem)
    load.start()

    barrier = pltpu.get_barrier_semaphore()
    for offset in range(1, n_space):
        pl.semaphore_signal(barrier, inc=1, device_id=(space_peer(offset), me_o), device_id_type=MESH)
    for offset in range(1, n_orb):
        pl.semaphore_signal(barrier, inc=1, device_id=(me_s, orb_peer(offset)), device_id_type=MESH)
    pl.semaphore_wait(barrier, n_space + n_orb - 2)

    def halo(half, step, chunk, side):
        start, landing = ((REACH, REACH + planes), (planes, 0))[side]
        ys = pl.ds(chunk * rows, rows)
        return remote(
            fields.at[half, step, pl.ds(start, REACH), ys],
            fields.at[half, step, pl.ds(landing, REACH), ys],
            halo_send.at[half, step, chunk, side],
            halo_recv.at[half, step, chunk, side],
            (left, right)[side],
            me_o,
        )

    def outward(half, chunk, offset):
        peer = orb_peer(offset)
        return remote(
            last.at[half, pl.ds(peer * share, share), pl.ds(chunk * rows, rows)],
            mixed.at[half, chunk, :, :, :, lane_block(me_o)],
            to_send.at[half, chunk, offset],
            to_recv.at[half, chunk, offset],
            me_s,
            peer,
        )

    def outward_own(half, chunk):
        return pltpu.make_async_copy(
            last.at[half, pl.ds(me_o * share, share), pl.ds(chunk * rows, rows)],
            mixed.at[half, chunk, :, :, :, lane_block(me_o)],
            to_own.at[half, chunk],
        )

    def gather(half, chunk, offset, turn_at):
        peer = orb_peer(offset)
        owner = lax.rem(peer + turn_at, n_orb)
        return remote(
            last.at[half, pl.ds(owner * share, share), pl.ds(chunk * rows, rows)],
            extra.at[half, chunk, turn_at, :, :, :, lane_block(me_o)],
            extra_send.at[half, chunk, offset, turn_at],
            extra_recv.at[half, chunk, offset, turn_at],
            me_s,
            peer,
        )

    def gather_start(half, chunk):
        for turn_at in range(1, n_orb):
            for offset in range(1, n_orb):
                gather(half, chunk, offset, turn_at).start()

    def back(chunk, offset):
        peer = orb_peer(offset)
        return remote(
            white.at[chunk - GATHERED, :, :, :, lane_block(peer)],
            out_ref.at[pl.ds(me_o * share, share), pl.ds(chunk * rows, rows)],
            back_send.at[chunk, offset],
            back_recv.at[chunk, offset],
            me_s,
            peer,
        )

    def back_own_copy(chunk):
        return pltpu.make_async_copy(
            white.at[chunk - GATHERED, :, :, :, lane_block(me_o)],
            out_ref.at[pl.ds(me_o * share, share), pl.ds(chunk * rows, rows)],
            back_own.at[chunk],
        )

    load.wait()
    first_lanes = lax.broadcasted_iota(jnp.int32, (deep, lanes), 1) < turn
    sublane = lax.broadcasted_iota(jnp.int32, (8, lanes), 0)

    def turned(value):
        return pltpu.roll(value, turn, value.ndim - 1)

    @pl.loop(0, planes)
    def _(plane):
        @pl.loop(0, ny)
        def _(y):
            top, bottom = raw[plane, y, :deep], raw[plane, y, deep:]
            fields[0, 0, plane + REACH, y] = jnp.where(first_lanes, top, turned(bottom))
            fields[1, 0, plane + REACH, y] = jnp.where(first_lanes, turned(top), bottom)

    def send_halos(half, step):
        @pl.loop(0, CHUNKS)
        def _(chunk):
            halo(half, step, chunk, 0).start()
            halo(half, step, chunk, 1).start()

    def along_depth(here):
        other = turned(here)
        inner = [here[i : i + 8] for i in range(0, deep, 8)]
        groups = [other[deep - 8 :]] + inner + [other[:8]]
        sums = []
        for k in range(1, REACH + 1):
            up = [pltpu.roll(group, k, 0) for group in groups[:-1]]
            down = [pltpu.roll(group, 8 - k, 0) for group in groups[1:]]
            sums.append(
                jnp.concatenate(
                    [
                        jnp.where(sublane < k, up[i], up[i + 1])
                        + jnp.where(sublane >= 8 - k, down[i + 1], down[i])
                        for i in range(len(inner))
                    ],
                    axis=0,
                )
            )
        return sums

    def filter_step(half, step):
        scale = (1.0 if step == 0 else 2.0) / HALF_WIDTH
        weights = [-0.5 * scale * w for w in STENCIL_WEIGHTS]

        @pl.loop(0, CHUNKS)
        def _(chunk):
            halo(half, step, chunk, 0).wait_recv()
            halo(half, step, chunk, 1).wait_recv()

            @pl.loop(0, planes)
            def _(plane):
                at = plane + REACH
                for row in range(rows):
                    y = chunk * rows + row
                    here = fields[half, step, at, y]
                    value = (scale * coef_ref[plane, y]) * here
                    depth = along_depth(here)
                    for k in range(1, REACH + 1):
                        along = (fields[half, step, at + k, y] + fields[half, step, at - k, y]) + (
                            fields[half, step, at, lax.rem(y + k, ny)]
                            + fields[half, step, at, lax.rem(y + (ny - k), ny)]
                        )
                        value = value + weights[k] * (along + depth[k - 1])
                    if step > 0:
                        value = value - fields[half, step - 1, at, y]
                    if step < DEGREE - 1:
                        fields[half, step + 1, at, y] = value
                    else:
                        last[half, plane, y] = value

            if step < DEGREE - 1:
                halo(half, step + 1, chunk, 0).start()
                halo(half, step + 1, chunk, 1).start()
            else:
                for offset in range(1, n_orb):
                    outward(half, chunk, offset).start()
                outward_own(half, chunk).start()

    send_halos(0, 0)

    @pl.loop(0, planes)
    def _(plane):
        levels = potential_ref[plane] - (CENTER + 1.5 * STENCIL_WEIGHTS[0])
        for y in range(ny):
            front = jnp.broadcast_to(levels[:, y : y + 1], (deep, lanes))
            rear = jnp.broadcast_to(levels[:, ny + y : ny + y + 1], (deep, lanes))
            coef_ref[plane, y] = jnp.where(first_lanes, front, rear)

    for step in range(DEGREE - 2):
        filter_step(0, step)
    send_halos(1, 0)
    filter_step(0, DEGREE - 2)
    filter_step(1, 0)
    filter_step(0, DEGREE - 1)
    for step in range(1, DEGREE):
        filter_step(1, step)

    gather_start(0, 0)

    def unpacked(one, two):
        shape = (share * rows, deep, lanes)
        one, two = one.reshape(shape), two.reshape(shape)
        lower = lax.broadcasted_iota(jnp.int32, shape, 2) < turn
        whole = jnp.concatenate(
            [jnp.where(lower, one, turned(two)), jnp.where(lower, turned(one), two)], axis=1
        )
        return split(whole.reshape(cells, lanes))

    part[...] = jnp.zeros_like(part)
    cross[...] = jnp.zeros_like(cross)

    @pl.loop(0, CHUNKS)
    def _(chunk):
        at = pl.ds(pl.multiple_of(chunk * cells, cells), cells)
        for half in range(2):
            for offset in range(1, n_orb):
                outward(half, chunk, offset).wait_recv()
            outward_own(half, chunk).wait()
        for block in range(n_orb):
            columns = pl.ds(block * lanes, lanes)
            high[at, columns], low[at, columns] = unpacked(
                mixed[0, chunk, :, :, :, columns], mixed[1, chunk, :, :, :, columns]
            )
        head, tail = high[at], low[at]
        part[...] += transposed_dot(head, head)
        cross[...] += transposed_dot(head, tail)

    part[...] = (part[...] + 2.0 * cross[...]) * (1.0 / (CHUNKS * cells * n_space * n_orb))

    def send_rows(offset):
        peer = space_peer(offset)
        return remote(
            part.at[row_block(peer)], landed.at[offset - 1],
            rows_send.at[offset], rows_recv.at[offset], peer, me_o,
        )

    def send_cols(offset):
        peer = orb_peer(offset)
        return remote(
            summed.at[:, lane_block(peer)], landed_cols.at[offset - 1],
            cols_send.at[offset], cols_recv.at[offset], me_s, peer,
        )

    def gather_cols(offset):
        block = total.at[row_block(me_s), lane_block(me_o)]
        return remote(block, block, gcols_send.at[offset], gcols_recv.at[offset], me_s, orb_peer(offset))

    def gather_rows(offset):
        block = total.at[row_block(me_s)]
        return remote(block, block, grows_send.at[offset], grows_recv.at[offset], space_peer(offset), me_o)

    for offset in range(1, n_space):
        send_rows(offset).start()
    value = part[row_block(me_s)]
    for offset in range(1, n_space):
        send_rows(offset).wait_recv()
        value = value + landed[offset - 1]
    summed[...] = value
    for offset in range(1, n_orb):
        send_cols(offset).start()
    value = summed[:, lane_block(me_o)]
    for offset in range(1, n_orb):
        send_cols(offset).wait_recv()
        value = value + landed_cols[offset - 1]
    total[row_block(me_s), lane_block(me_o)] = value
    for offset in range(1, n_orb):
        gather_cols(offset).start()
    for offset in range(1, n_orb):
        gather_cols(offset).wait_recv()
    for offset in range(1, n_space):
        gather_rows(offset).start()
    for chunk in range(GATHERED):
        for half in range(2):
            if (half, chunk) != (0, 0):
                gather_start(half, chunk)
    for offset in range(1, n_space):
        gather_rows(offset).wait_recv()

    one_sided = total[...]
    intersection = 0.5 * (one_sided + one_sided.T)
    squares = jnp.sum(intersection * intersection, axis=0, keepdims=True)
    norm_scale = jnp.sqrt(jnp.sum(squares, axis=1, keepdims=True) + 1e-06)
    on_diagonal = lax.broadcasted_iota(jnp.int32, (norb, norb), 0) == lax.broadcasted_iota(
        jnp.int32, (norb, norb), 1
    )

    def factor_of(term):
        return jnp.where(on_diagonal, 1.5, 0.0) - 0.5 * term

    scaled = intersection / norm_scale
    inverse = factor_of(scaled)
    z_ref[...] = inverse
    y_ref[...] = product(split(scaled), split(inverse))

    @pl.loop(1, NS_ITERS - 1)
    def _(step):
        ys, zs = split(y_ref[...]), split(z_ref[...])
        fs = split(factor_of(product(zs, ys)))
        y_ref[...] = product(ys, fs)
        z_ref[...] = product(fs, zs)

    ys, zs = split(y_ref[...]), split(z_ref[...])
    fs = split(factor_of(product(zs, ys)))
    z_ref[...] = product(fs, zs) / jnp.sqrt(norm_scale)

    @pl.loop(GATHERED, CHUNKS)
    def _(chunk):
        at = pl.ds(pl.multiple_of(chunk * cells, cells), cells)
        value = product((high[at], low[at]), split(z_ref[...]))
        white[chunk - GATHERED] = value.reshape(share, rows, nz, norb)
        for offset in range(1, n_orb):
            back(chunk, offset).start()
        back_own_copy(chunk).start()

    own = split(z_ref[:, lane_block(me_o)])

    for chunk in range(GATHERED):
        at = pl.ds(chunk * cells, cells)
        ys = pl.ds(chunk * rows, rows)
        value = product((high[at], low[at]), own)
        out_ref[pl.ds(me_o * share, share), ys] = value.reshape(share, rows, nz, lanes)
        for turn_at in range(1, n_orb):
            owned = pl.ds(lax.rem(me_o + turn_at, n_orb) * share, share)
            for half in range(2):
                for offset in range(1, n_orb):
                    gather(half, chunk, offset, turn_at).wait_recv()
                extra[half, chunk, turn_at, :, :, :, lane_block(me_o)] = last[half, owned, ys]
            parts = []
            for block in range(n_orb):
                columns = pl.ds(block * lanes, lanes)
                parts.append(
                    unpacked(
                        extra[0, chunk, turn_at, :, :, :, columns],
                        extra[1, chunk, turn_at, :, :, :, columns],
                    )
                )
            field = tuple(jnp.concatenate([p[i] for p in parts], axis=1) for i in range(2))
            out_ref[owned, ys] = product(field, own).reshape(share, rows, nz, lanes)

    for offset in range(1, n_space):
        send_rows(offset).wait_send()
        gather_rows(offset).wait_send()
    for offset in range(1, n_orb):
        send_cols(offset).wait_send()
        gather_cols(offset).wait_send()
    for half in range(2):
        for step in range(DEGREE):

            @pl.loop(0, CHUNKS)
            def _(chunk):
                halo(half, step, chunk, 0).wait_send()
                halo(half, step, chunk, 1).wait_send()

    @pl.loop(0, CHUNKS)
    def _(chunk):
        for offset in range(1, n_orb):
            outward(0, chunk, offset).wait_send()
            outward(1, chunk, offset).wait_send()

    for chunk in range(GATHERED):
        for half in range(2):
            for turn_at in range(1, n_orb):
                for offset in range(1, n_orb):
                    gather(half, chunk, offset, turn_at).wait_send()

    @pl.loop(GATHERED, CHUNKS)
    def _(chunk):
        back_own_copy(chunk).wait()
        for offset in range(1, n_orb):
            back(chunk, offset).wait()


def body(n_space, n_orb, orbitals, potential):
    planes, ny, nz, lanes = orbitals.shape
    norb = lanes * n_orb
    piece = norb // n_space
    block = (CHUNKS, planes // n_orb, ny // CHUNKS, nz, norb)
    cells = planes * ny * nz // n_orb
    by_depth = jnp.transpose(potential.reshape(planes, ny, 2, nz // 2), (0, 3, 2, 1))
    by_depth = by_depth.reshape(planes, nz // 2, 2 * ny)
    f32 = jnp.float32
    dma = pltpu.SemaphoreType.DMA
    return pl.pallas_call(
        functools.partial(kernel, n_space, n_orb),
        out_shape=jax.ShapeDtypeStruct(orbitals.shape, f32),
        in_specs=[pl.BlockSpec(memory_space=pl.ANY), pl.BlockSpec(memory_space=pltpu.VMEM)],
        out_specs=pl.BlockSpec(memory_space=pltpu.VMEM),
        scratch_shapes=[
            pltpu.VMEM((planes, ny, nz, lanes), f32),
            pltpu.VMEM((planes, ny, nz // 2, lanes), f32),
            pltpu.VMEM((2, DEGREE, planes + 2 * REACH, ny, nz // 2, lanes), f32),
            pltpu.VMEM((2, planes, ny, nz // 2, lanes), f32),
            pltpu.VMEM((2,) + block[:3] + (nz // 2, norb), f32),
            pltpu.VMEM((2, GATHERED, n_orb) + block[1:3] + (nz // 2, norb), f32),
            pltpu.VMEM((cells, norb), jnp.bfloat16),
            pltpu.VMEM((cells, norb), jnp.bfloat16),
            pltpu.VMEM((norb, norb), f32),
            pltpu.VMEM((norb, norb), f32),
            pltpu.VMEM((n_space - 1, piece, norb), f32),
            pltpu.VMEM((piece, norb), f32),
            pltpu.VMEM((n_orb - 1, piece, lanes), f32),
            pltpu.VMEM((norb, norb), f32),
            pltpu.VMEM((norb, norb), f32),
            pltpu.VMEM((norb, norb), f32),
            pltpu.VMEM((CHUNKS - GATHERED,) + block[1:], f32),
            dma,
            dma((2, DEGREE, CHUNKS, 2)),
            dma((2, DEGREE, CHUNKS, 2)),
            dma((2, CHUNKS, n_orb)),
            dma((2, CHUNKS, n_orb)),
            dma((2, CHUNKS)),
            dma((2, GATHERED, n_orb, n_orb)),
            dma((2, GATHERED, n_orb, n_orb)),
            dma((n_space,)),
            dma((n_space,)),
            dma((n_orb,)),
            dma((n_orb,)),
            dma((n_orb,)),
            dma((n_orb,)),
            dma((n_space,)),
            dma((n_space,)),
            dma((CHUNKS, n_orb)),
            dma((CHUNKS, n_orb)),
            dma((CHUNKS,)),
        ],
        compiler_params=pltpu.CompilerParams(
            collective_id=0, has_side_effects=True, vmem_limit_bytes=60 * 1024 * 1024
        ),
        cost_estimate=pl.CostEstimate(
            flops=20_000_000_000, bytes_accessed=8_000_000, transcendentals=0
        ),
    )(orbitals, by_depth)


def solution(mesh):
    return jax.shard_map(
        functools.partial(body, mesh.shape["space"], mesh.shape["orb"]),
        mesh=mesh,
        in_specs=(P("space", None, None, "orb"), P("space", None, None)),
        out_specs=P("space", None, None, "orb"),
        check_vma=False,
    )
```

```python
import functools

import jax
import jax.numpy as jnp
from jax import lax
from jax.experimental import pallas as pl
from jax.experimental.pallas import tpu as pltpu
from jax.sharding import PartitionSpec as P

DEGREE = 4
NS_ITERS = 8

STENCIL_WEIGHTS = [-49.0 / 18.0, 3.0 / 2.0, -3.0 / 20.0, 1.0 / 90.0]
CENTER = 5.0
HALF_WIDTH = 4.0
REACH = 3
CHUNKS = 4
GATHERED = 1
MESH = pl.DeviceIdType.MESH


def split(value):
    high = value.astype(jnp.bfloat16)
    low = (value - high.astype(jnp.float32)).astype(jnp.bfloat16)
    return high, low


def product(left, right):
    return jnp.dot(
        jnp.concatenate([left[0], left[0], left[1]], axis=1),
        jnp.concatenate([right[0], right[1], right[0]], axis=0),
        preferred_element_type=jnp.float32,
    )


def transposed_dot(left, right):
    return lax.dot_general(
        left, right, (((0,), (0,)), ((), ())), preferred_element_type=jnp.float32
    )


def kernel(
    n_space, n_orb, x_ref, potential_ref, out_ref,
    raw, coef_ref, fields, last, mixed, extra, high, low, part, cross, landed_half, landed, summed, landed_cols, total, y_ref, z_ref, white,
    load_sem, halo_send, halo_recv, to_send, to_recv, to_own, extra_send, extra_recv,
    half_send, half_recv, ghalf_send, ghalf_recv,
    rows_send, rows_recv, cols_send, cols_recv, gcols_send, gcols_recv, grows_send, grows_recv,
    back_send, back_recv, back_own,
):
    planes, ny, nz, lanes = x_ref.shape
    norb = total.shape[0]
    rows = ny // CHUNKS
    share = planes // n_orb
    cells = share * rows * nz
    deep = nz // 2
    turn = lanes // 2
    piece = norb // n_space
    me_s = lax.axis_index("space")
    me_o = lax.axis_index("orb")
    left = lax.rem(me_s + n_space - 1, n_space)
    right = lax.rem(me_s + 1, n_space)

    def space_peer(offset):
        return lax.rem(me_s + offset, n_space)

    def orb_peer(offset):
        return lax.rem(me_o + offset, n_orb)

    n_pair = n_space // 2
    core = lax.rem(me_s, 2)
    pair = me_s // 2

    def core_rows(at):
        return pl.ds(pl.multiple_of(at * (n_pair * piece), n_pair * piece), n_pair * piece)

    def row_block(at):
        return pl.ds(pl.multiple_of((core * n_pair + at) * piece, piece), piece)

    def lane_block(device):
        return pl.ds(pl.multiple_of(device * lanes, lanes), lanes)

    def remote(src, dst, send, recv, space, orb):
        return pltpu.make_async_remote_copy(
            src_ref=src, dst_ref=dst, send_sem=send, recv_sem=recv,
            device_id=(space, orb), device_id_type=MESH,
        )

    load = pltpu.make_async_copy(x_ref, raw, load_sem)
    load.start()

    barrier = pltpu.get_barrier_semaphore()
    for offset in range(1, n_space):
        pl.semaphore_signal(barrier, inc=1, device_id=(space_peer(offset), me_o), device_id_type=MESH)
    for offset in range(1, n_orb):
        pl.semaphore_signal(barrier, inc=1, device_id=(me_s, orb_peer(offset)), device_id_type=MESH)
    pl.semaphore_wait(barrier, n_space + n_orb - 2)

    def halo(half, step, chunk, side):
        start, landing = ((REACH, REACH + planes), (planes, 0))[side]
        ys = pl.ds(chunk * rows, rows)
        return remote(
            fields.at[half, step, pl.ds(start, REACH), ys],
            fields.at[half, step, pl.ds(landing, REACH), ys],
            halo_send.at[half, step, chunk, side],
            halo_recv.at[half, step, chunk, side],
            (left, right)[side],
            me_o,
        )

    def outward(half, chunk, offset):
        peer = orb_peer(offset)
        return remote(
            last.at[half, pl.ds(peer * share, share), pl.ds(chunk * rows, rows)],
            mixed.at[half, chunk, :, :, :, lane_block(me_o)],
            to_send.at[half, chunk, offset],
            to_recv.at[half, chunk, offset],
            me_s,
            peer,
        )

    def outward_own(half, chunk):
        return pltpu.make_async_copy(
            last.at[half, pl.ds(me_o * share, share), pl.ds(chunk * rows, rows)],
            mixed.at[half, chunk, :, :, :, lane_block(me_o)],
            to_own.at[half, chunk],
        )

    def gather(half, chunk, offset, turn_at):
        peer = orb_peer(offset)
        owner = lax.rem(peer + turn_at, n_orb)
        return remote(
            last.at[half, pl.ds(owner * share, share), pl.ds(chunk * rows, rows)],
            extra.at[half, chunk, turn_at, :, :, :, lane_block(me_o)],
            extra_send.at[half, chunk, offset, turn_at],
            extra_recv.at[half, chunk, offset, turn_at],
            me_s,
            peer,
        )

    def gather_start(half, chunk):
        for turn_at in range(1, n_orb):
            for offset in range(1, n_orb):
                gather(half, chunk, offset, turn_at).start()

    def back(chunk, offset):
        peer = orb_peer(offset)
        return remote(
            white.at[chunk - GATHERED, :, :, :, lane_block(peer)],
            out_ref.at[pl.ds(me_o * share, share), pl.ds(chunk * rows, rows)],
            back_send.at[chunk, offset],
            back_recv.at[chunk, offset],
            me_s,
            peer,
        )

    def back_own_copy(chunk):
        return pltpu.make_async_copy(
            white.at[chunk - GATHERED, :, :, :, lane_block(me_o)],
            out_ref.at[pl.ds(me_o * share, share), pl.ds(chunk * rows, rows)],
            back_own.at[chunk],
        )

    load.wait()
    first_lanes = lax.broadcasted_iota(jnp.int32, (deep, lanes), 1) < turn
    sublane = lax.broadcasted_iota(jnp.int32, (8, lanes), 0)

    def turned(value):
        return pltpu.roll(value, turn, value.ndim - 1)

    @pl.loop(0, planes)
    def _(plane):
        @pl.loop(0, ny)
        def _(y):
            top, bottom = raw[plane, y, :deep], raw[plane, y, deep:]
            fields[0, 0, plane + REACH, y] = jnp.where(first_lanes, top, turned(bottom))
            fields[1, 0, plane + REACH, y] = jnp.where(first_lanes, turned(top), bottom)

    def send_halos(half, step):
        @pl.loop(0, CHUNKS)
        def _(chunk):
            halo(half, step, chunk, 0).start()
            halo(half, step, chunk, 1).start()

    def along_depth(here):
        other = turned(here)
        inner = [here[i : i + 8] for i in range(0, deep, 8)]
        groups = [other[deep - 8 :]] + inner + [other[:8]]
        sums = []
        for k in range(1, REACH + 1):
            up = [pltpu.roll(group, k, 0) for group in groups[:-1]]
            down = [pltpu.roll(group, 8 - k, 0) for group in groups[1:]]
            sums.append(
                jnp.concatenate(
                    [
                        jnp.where(sublane < k, up[i], up[i + 1])
                        + jnp.where(sublane >= 8 - k, down[i + 1], down[i])
                        for i in range(len(inner))
                    ],
                    axis=0,
                )
            )
        return sums

    def filter_step(half, step):
        scale = (1.0 if step == 0 else 2.0) / HALF_WIDTH
        weights = [-0.5 * scale * w for w in STENCIL_WEIGHTS]

        @pl.loop(0, CHUNKS)
        def _(chunk):
            halo(half, step, chunk, 0).wait_recv()
            halo(half, step, chunk, 1).wait_recv()

            @pl.loop(0, planes)
            def _(plane):
                at = plane + REACH
                for row in range(rows):
                    y = chunk * rows + row
                    here = fields[half, step, at, y]
                    value = (scale * coef_ref[plane, y]) * here
                    depth = along_depth(here)
                    for k in range(1, REACH + 1):
                        along = (fields[half, step, at + k, y] + fields[half, step, at - k, y]) + (
                            fields[half, step, at, lax.rem(y + k, ny)]
                            + fields[half, step, at, lax.rem(y + (ny - k), ny)]
                        )
                        value = value + weights[k] * (along + depth[k - 1])
                    if step > 0:
                        value = value - fields[half, step - 1, at, y]
                    if step < DEGREE - 1:
                        fields[half, step + 1, at, y] = value
                    else:
                        last[half, plane, y] = value

            if step < DEGREE - 1:
                halo(half, step + 1, chunk, 0).start()
                halo(half, step + 1, chunk, 1).start()
            else:
                for offset in range(1, n_orb):
                    outward(half, chunk, offset).start()
                outward_own(half, chunk).start()

    send_halos(0, 0)

    @pl.loop(0, planes)
    def _(plane):
        levels = potential_ref[plane] - (CENTER + 1.5 * STENCIL_WEIGHTS[0])
        for y in range(ny):
            front = jnp.broadcast_to(levels[:, y : y + 1], (deep, lanes))
            rear = jnp.broadcast_to(levels[:, ny + y : ny + y + 1], (deep, lanes))
            coef_ref[plane, y] = jnp.where(first_lanes, front, rear)

    for step in range(DEGREE - 2):
        filter_step(0, step)
    send_halos(1, 0)
    filter_step(0, DEGREE - 2)
    filter_step(1, 0)
    filter_step(0, DEGREE - 1)
    for step in range(1, DEGREE):
        filter_step(1, step)

    def unpacked(one, two):
        shape = (share * rows, deep, lanes)
        one, two = one.reshape(shape), two.reshape(shape)
        lower = lax.broadcasted_iota(jnp.int32, shape, 2) < turn
        whole = jnp.concatenate(
            [jnp.where(lower, one, turned(two)), jnp.where(lower, turned(one), two)], axis=1
        )
        return split(whole.reshape(cells, lanes))

    part[...] = jnp.zeros_like(part)
    cross[...] = jnp.zeros_like(cross)

    @pl.loop(0, CHUNKS)
    def _(chunk):
        at = pl.ds(pl.multiple_of(chunk * cells, cells), cells)
        for half in range(2):
            for offset in range(1, n_orb):
                outward(half, chunk, offset).wait_recv()
            outward_own(half, chunk).wait()
        for block in range(n_orb):
            columns = pl.ds(block * lanes, lanes)
            high[at, columns], low[at, columns] = unpacked(
                mixed[0, chunk, :, :, :, columns], mixed[1, chunk, :, :, :, columns]
            )
        head, tail = high[at], low[at]
        part[...] += transposed_dot(head, head)
        cross[...] += transposed_dot(head, tail)

    part[...] = (part[...] + 2.0 * cross[...]) * (1.0 / (CHUNKS * cells * n_space * n_orb))

    def pair_peer(offset):
        return lax.rem(pair + offset, n_pair)

    def send_half():
        return remote(
            part.at[core_rows(1 - core)], landed_half, half_send, half_recv, 2 * pair + 1 - core, me_o
        )

    def send_rows(offset):
        peer = pair_peer(offset)
        return remote(
            part.at[row_block(peer)], landed.at[offset - 1],
            rows_send.at[offset], rows_recv.at[offset], 2 * peer + core, me_o,
        )

    def send_cols(offset):
        peer = orb_peer(offset)
        return remote(
            summed.at[:, lane_block(peer)], landed_cols.at[offset - 1],
            cols_send.at[offset], cols_recv.at[offset], me_s, peer,
        )

    def gather_cols(offset):
        block = total.at[row_block(pair), lane_block(me_o)]
        return remote(block, block, gcols_send.at[offset], gcols_recv.at[offset], me_s, orb_peer(offset))

    def gather_rows(offset):
        block = total.at[row_block(pair)]
        return remote(
            block, block, grows_send.at[offset], grows_recv.at[offset], 2 * pair_peer(offset) + core, me_o
        )

    def gather_half():
        block = total.at[core_rows(core)]
        return remote(block, block, ghalf_send, ghalf_recv, 2 * pair + 1 - core, me_o)

    send_half().start()
    send_half().wait_recv()
    part[core_rows(core)] += landed_half[...]
    for offset in range(1, n_pair):
        send_rows(offset).start()
    value = part[row_block(pair)]
    for offset in range(1, n_pair):
        send_rows(offset).wait_recv()
        value = value + landed[offset - 1]
    summed[...] = value
    for offset in range(1, n_orb):
        send_cols(offset).start()
    value = summed[:, lane_block(me_o)]
    for offset in range(1, n_orb):
        send_cols(offset).wait_recv()
        value = value + landed_cols[offset - 1]
    total[row_block(pair), lane_block(me_o)] = value
    for offset in range(1, n_orb):
        gather_cols(offset).start()
    for offset in range(1, n_orb):
        gather_cols(offset).wait_recv()
    for offset in range(1, n_pair):
        gather_rows(offset).start()
    for chunk in range(GATHERED):
        for half in range(2):
            gather_start(half, chunk)
    for offset in range(1, n_pair):
        gather_rows(offset).wait_recv()
    gather_half().start()
    gather_half().wait_recv()

    one_sided = total[...]
    intersection = 0.5 * (one_sided + one_sided.T)
    squares = jnp.sum(intersection * intersection, axis=0, keepdims=True)
    norm_scale = jnp.sqrt(jnp.sum(squares, axis=1, keepdims=True) + 1e-06)
    on_diagonal = lax.broadcasted_iota(jnp.int32, (norb, norb), 0) == lax.broadcasted_iota(
        jnp.int32, (norb, norb), 1
    )

    def factor_of(term):
        return jnp.where(on_diagonal, 1.5, 0.0) - 0.5 * term

    scaled = intersection / norm_scale
    inverse = factor_of(scaled)
    z_ref[...] = inverse
    y_ref[...] = product(split(scaled), split(inverse))

    @pl.loop(1, NS_ITERS - 1)
    def _(step):
        ys, zs = split(y_ref[...]), split(z_ref[...])
        fs = split(factor_of(product(zs, ys)))
        y_ref[...] = product(ys, fs)
        z_ref[...] = product(fs, zs)

    ys, zs = split(y_ref[...]), split(z_ref[...])
    fs = split(factor_of(product(zs, ys)))
    z_ref[...] = product(fs, zs) / jnp.sqrt(norm_scale)

    @pl.loop(GATHERED, CHUNKS)
    def _(chunk):
        at = pl.ds(pl.multiple_of(chunk * cells, cells), cells)
        value = product((high[at], low[at]), split(z_ref[...]))
        white[chunk - GATHERED] = value.reshape(share, rows, nz, norb)
        for offset in range(1, n_orb):
            back(chunk, offset).start()
        back_own_copy(chunk).start()

    own = split(z_ref[:, lane_block(me_o)])

    for chunk in range(GATHERED):
        at = pl.ds(chunk * cells, cells)
        ys = pl.ds(chunk * rows, rows)
        value = product((high[at], low[at]), own)
        out_ref[pl.ds(me_o * share, share), ys] = value.reshape(share, rows, nz, lanes)
        for turn_at in range(1, n_orb):
            owned = pl.ds(lax.rem(me_o + turn_at, n_orb) * share, share)
            for half in range(2):
                for offset in range(1, n_orb):
                    gather(half, chunk, offset, turn_at).wait_recv()
                extra[half, chunk, turn_at, :, :, :, lane_block(me_o)] = last[half, owned, ys]
            parts = []
            for block in range(n_orb):
                columns = pl.ds(block * lanes, lanes)
                parts.append(
                    unpacked(
                        extra[0, chunk, turn_at, :, :, :, columns],
                        extra[1, chunk, turn_at, :, :, :, columns],
                    )
                )
            field = tuple(jnp.concatenate([p[i] for p in parts], axis=1) for i in range(2))
            out_ref[owned, ys] = product(field, own).reshape(share, rows, nz, lanes)

    send_half().wait_send()
    gather_half().wait_send()
    for offset in range(1, n_pair):
        send_rows(offset).wait_send()
        gather_rows(offset).wait_send()
    for offset in range(1, n_orb):
        send_cols(offset).wait_send()
        gather_cols(offset).wait_send()
    for half in range(2):
        for step in range(DEGREE):

            @pl.loop(0, CHUNKS)
            def _(chunk):
                halo(half, step, chunk, 0).wait_send()
                halo(half, step, chunk, 1).wait_send()

    @pl.loop(0, CHUNKS)
    def _(chunk):
        for offset in range(1, n_orb):
            outward(0, chunk, offset).wait_send()
            outward(1, chunk, offset).wait_send()

    for chunk in range(GATHERED):
        for half in range(2):
            for turn_at in range(1, n_orb):
                for offset in range(1, n_orb):
                    gather(half, chunk, offset, turn_at).wait_send()

    @pl.loop(GATHERED, CHUNKS)
    def _(chunk):
        back_own_copy(chunk).wait()
        for offset in range(1, n_orb):
            back(chunk, offset).wait()


def body(n_space, n_orb, orbitals, potential):
    planes, ny, nz, lanes = orbitals.shape
    norb = lanes * n_orb
    piece = norb // n_space
    block = (CHUNKS, planes // n_orb, ny // CHUNKS, nz, norb)
    cells = planes * ny * nz // n_orb
    by_depth = jnp.transpose(potential.reshape(planes, ny, 2, nz // 2), (0, 3, 2, 1))
    by_depth = by_depth.reshape(planes, nz // 2, 2 * ny)
    f32 = jnp.float32
    dma = pltpu.SemaphoreType.DMA
    return pl.pallas_call(
        functools.partial(kernel, n_space, n_orb),
        out_shape=jax.ShapeDtypeStruct(orbitals.shape, f32),
        in_specs=[pl.BlockSpec(memory_space=pl.ANY), pl.BlockSpec(memory_space=pltpu.VMEM)],
        out_specs=pl.BlockSpec(memory_space=pltpu.VMEM),
        scratch_shapes=[
            pltpu.VMEM((planes, ny, nz, lanes), f32),
            pltpu.VMEM((planes, ny, nz // 2, lanes), f32),
            pltpu.VMEM((2, DEGREE, planes + 2 * REACH, ny, nz // 2, lanes), f32),
            pltpu.VMEM((2, planes, ny, nz // 2, lanes), f32),
            pltpu.VMEM((2,) + block[:3] + (nz // 2, norb), f32),
            pltpu.VMEM((2, GATHERED, n_orb) + block[1:3] + (nz // 2, norb), f32),
            pltpu.VMEM((cells, norb), jnp.bfloat16),
            pltpu.VMEM((cells, norb), jnp.bfloat16),
            pltpu.VMEM((norb, norb), f32),
            pltpu.VMEM((norb, norb), f32),
            pltpu.VMEM((norb // 2, norb), f32),
            pltpu.VMEM((n_space // 2 - 1, piece, norb), f32),
            pltpu.VMEM((piece, norb), f32),
            pltpu.VMEM((n_orb - 1, piece, lanes), f32),
            pltpu.VMEM((norb, norb), f32),
            pltpu.VMEM((norb, norb), f32),
            pltpu.VMEM((norb, norb), f32),
            pltpu.VMEM((CHUNKS - GATHERED,) + block[1:], f32),
            dma,
            dma((2, DEGREE, CHUNKS, 2)),
            dma((2, DEGREE, CHUNKS, 2)),
            dma((2, CHUNKS, n_orb)),
            dma((2, CHUNKS, n_orb)),
            dma((2, CHUNKS)),
            dma((2, GATHERED, n_orb, n_orb)),
            dma((2, GATHERED, n_orb, n_orb)),
            dma,
            dma,
            dma,
            dma,
            dma((n_space // 2,)),
            dma((n_space // 2,)),
            dma((n_orb,)),
            dma((n_orb,)),
            dma((n_orb,)),
            dma((n_orb,)),
            dma((n_space // 2,)),
            dma((n_space // 2,)),
            dma((CHUNKS, n_orb)),
            dma((CHUNKS, n_orb)),
            dma((CHUNKS,)),
        ],
        compiler_params=pltpu.CompilerParams(
            collective_id=0, has_side_effects=True, vmem_limit_bytes=60 * 1024 * 1024
        ),
        cost_estimate=pl.CostEstimate(
            flops=20_000_000_000, bytes_accessed=8_000_000, transcendentals=0
        ),
    )(orbitals, by_depth)


def solution(mesh):
    return jax.shard_map(
        functools.partial(body, mesh.shape["space"], mesh.shape["orb"]),
        mesh=mesh,
        in_specs=(P("space", None, None, "orb"), P("space", None, None)),
        out_specs=P("space", None, None, "orb"),
        check_vma=False,
    )
```

```python
import functools

import jax
import jax.numpy as jnp
from jax import lax
from jax.experimental import pallas as pl
from jax.experimental.pallas import tpu as pltpu
from jax.sharding import PartitionSpec as P

DEGREE = 4
NS_ITERS = 8

STENCIL_WEIGHTS = [-49.0 / 18.0, 3.0 / 2.0, -3.0 / 20.0, 1.0 / 90.0]
CENTER = 5.0
HALF_WIDTH = 4.0
REACH = 3
CHUNKS = 4
GATHERED = 1
MESH = pl.DeviceIdType.MESH


def split(value):
    high = value.astype(jnp.bfloat16)
    low = (value - high.astype(jnp.float32)).astype(jnp.bfloat16)
    return high, low


def product(left, right):
    return jnp.dot(
        jnp.concatenate([left[0], left[0], left[1]], axis=1),
        jnp.concatenate([right[0], right[1], right[0]], axis=0),
        preferred_element_type=jnp.float32,
    )


def transposed_dot(left, right):
    return lax.dot_general(
        left, right, (((0,), (0,)), ((), ())), preferred_element_type=jnp.float32
    )


def kernel(
    n_space, n_orb, x_ref, potential_ref, out_ref,
    raw, coef_ref, fields, last, mixed, extra, high, low, part, cross, landed_half, landed, summed, landed_cols, total, y_ref, z_ref, white,
    load_sem, halo_send, halo_recv, to_send, to_recv, to_own, extra_send, extra_recv,
    half_send, half_recv, ghalf_send, ghalf_recv,
    rows_send, rows_recv, cols_send, cols_recv, gcols_send, gcols_recv, grows_send, grows_recv,
    back_send, back_recv, back_own,
):
    planes, ny, nz, lanes = x_ref.shape
    norb = total.shape[0]
    rows = ny // CHUNKS
    share = planes // n_orb
    cells = share * rows * nz
    deep = nz // 2
    turn = lanes // 2
    piece = norb // n_space
    me_s = lax.axis_index("space")
    me_o = lax.axis_index("orb")
    left = lax.rem(me_s + n_space - 1, n_space)
    right = lax.rem(me_s + 1, n_space)

    def space_peer(offset):
        return lax.rem(me_s + offset, n_space)

    def orb_peer(offset):
        return lax.rem(me_o + offset, n_orb)

    n_pair = n_space // 2
    core = lax.rem(me_s, 2)
    pair = me_s // 2

    def core_rows(at):
        return pl.ds(pl.multiple_of(at * (n_pair * piece), n_pair * piece), n_pair * piece)

    def row_block(at):
        return pl.ds(pl.multiple_of((core * n_pair + at) * piece, piece), piece)

    def lane_block(device):
        return pl.ds(pl.multiple_of(device * lanes, lanes), lanes)

    def remote(src, dst, send, recv, space, orb):
        return pltpu.make_async_remote_copy(
            src_ref=src, dst_ref=dst, send_sem=send, recv_sem=recv,
            device_id=(space, orb), device_id_type=MESH,
        )

    load = pltpu.make_async_copy(x_ref, raw, load_sem)
    load.start()

    barrier = pltpu.get_barrier_semaphore()
    for offset in range(1, n_space):
        pl.semaphore_signal(barrier, inc=1, device_id=(space_peer(offset), me_o), device_id_type=MESH)
    for offset in range(1, n_orb):
        pl.semaphore_signal(barrier, inc=1, device_id=(me_s, orb_peer(offset)), device_id_type=MESH)
    pl.semaphore_wait(barrier, n_space + n_orb - 2)

    def halo(half, step, chunk, side):
        start, landing = ((REACH, REACH + planes), (planes, 0))[side]
        ys = pl.ds(chunk * rows, rows)
        return remote(
            fields.at[half, step, pl.ds(start, REACH), ys],
            fields.at[half, step, pl.ds(landing, REACH), ys],
            halo_send.at[half, step, chunk, side],
            halo_recv.at[half, step, chunk, side],
            (left, right)[side],
            me_o,
        )

    def outward(half, chunk, offset):
        peer = orb_peer(offset)
        return remote(
            last.at[half, pl.ds(peer * share, share), pl.ds(chunk * rows, rows)],
            mixed.at[half, chunk, :, :, :, lane_block(me_o)],
            to_send.at[half, chunk, offset],
            to_recv.at[half, chunk, offset],
            me_s,
            peer,
        )

    def outward_own(half, chunk):
        return pltpu.make_async_copy(
            last.at[half, pl.ds(me_o * share, share), pl.ds(chunk * rows, rows)],
            mixed.at[half, chunk, :, :, :, lane_block(me_o)],
            to_own.at[half, chunk],
        )

    def gather(half, chunk, offset, turn_at):
        peer = orb_peer(offset)
        owner = lax.rem(peer + turn_at, n_orb)
        return remote(
            last.at[half, pl.ds(owner * share, share), pl.ds(chunk * rows, rows)],
            extra.at[half, chunk, turn_at, :, :, :, lane_block(me_o)],
            extra_send.at[half, chunk, offset, turn_at],
            extra_recv.at[half, chunk, offset, turn_at],
            me_s,
            peer,
        )

    def gather_start(half, chunk):
        for turn_at in range(1, n_orb):
            for offset in range(1, n_orb):
                gather(half, chunk, offset, turn_at).start()

    def back(chunk, offset):
        peer = orb_peer(offset)
        return remote(
            white.at[chunk - GATHERED, :, :, :, lane_block(peer)],
            out_ref.at[pl.ds(me_o * share, share), pl.ds(chunk * rows, rows)],
            back_send.at[chunk, offset],
            back_recv.at[chunk, offset],
            me_s,
            peer,
        )

    def back_own_copy(chunk):
        return pltpu.make_async_copy(
            white.at[chunk - GATHERED, :, :, :, lane_block(me_o)],
            out_ref.at[pl.ds(me_o * share, share), pl.ds(chunk * rows, rows)],
            back_own.at[chunk],
        )

    load.wait()
    first_lanes = lax.broadcasted_iota(jnp.int32, (deep, lanes), 1) < turn
    sublane = lax.broadcasted_iota(jnp.int32, (8, lanes), 0)

    def turned(value):
        return pltpu.roll(value, turn, value.ndim - 1)

    def pack(half):
        @pl.loop(0, planes)
        def _(plane):
            for y in range(ny):
                top, bottom = raw[plane, y, :deep], raw[plane, y, deep:]
                if half == 0:
                    value = jnp.where(first_lanes, top, turned(bottom))
                else:
                    value = jnp.where(first_lanes, turned(top), bottom)
                fields[half, 0, plane + REACH, y] = value

    def send_halos(half, step):
        @pl.loop(0, CHUNKS)
        def _(chunk):
            halo(half, step, chunk, 0).start()
            halo(half, step, chunk, 1).start()

    def along_depth(here):
        other = turned(here)
        inner = [here[i : i + 8] for i in range(0, deep, 8)]
        groups = [other[deep - 8 :]] + inner + [other[:8]]
        sums = []
        for k in range(1, REACH + 1):
            up = [pltpu.roll(group, k, 0) for group in groups[:-1]]
            down = [pltpu.roll(group, 8 - k, 0) for group in groups[1:]]
            sums.append(
                jnp.concatenate(
                    [
                        jnp.where(sublane < k, up[i], up[i + 1])
                        + jnp.where(sublane >= 8 - k, down[i + 1], down[i])
                        for i in range(len(inner))
                    ],
                    axis=0,
                )
            )
        return sums

    def filter_step(half, step):
        scale = (1.0 if step == 0 else 2.0) / HALF_WIDTH
        weights = [-0.5 * scale * w for w in STENCIL_WEIGHTS]

        @pl.loop(0, CHUNKS)
        def _(chunk):
            halo(half, step, chunk, 0).wait_recv()
            halo(half, step, chunk, 1).wait_recv()

            @pl.loop(0, planes, unroll=2)
            def _(plane):
                at = plane + REACH
                for row in range(rows):
                    y = chunk * rows + row
                    here = fields[half, step, at, y]
                    value = (scale * coef_ref[plane, y]) * here
                    depth = along_depth(here)
                    for k in range(1, REACH + 1):
                        along = (fields[half, step, at + k, y] + fields[half, step, at - k, y]) + (
                            fields[half, step, at, lax.rem(y + k, ny)]
                            + fields[half, step, at, lax.rem(y + (ny - k), ny)]
                        )
                        value = value + weights[k] * (along + depth[k - 1])
                    if step > 0:
                        value = value - fields[half, step - 1, at, y]
                    if step < DEGREE - 1:
                        fields[half, step + 1, at, y] = value
                    else:
                        last[half, plane, y] = value

            if step < DEGREE - 1:
                halo(half, step + 1, chunk, 0).start()
                halo(half, step + 1, chunk, 1).start()
            else:
                for offset in range(1, n_orb):
                    outward(half, chunk, offset).start()
                outward_own(half, chunk).start()

    pack(0)
    send_halos(0, 0)
    pack(1)

    @pl.loop(0, planes)
    def _(plane):
        levels = potential_ref[plane] - (CENTER + 1.5 * STENCIL_WEIGHTS[0])
        for y in range(ny):
            front = jnp.broadcast_to(levels[:, y : y + 1], (deep, lanes))
            rear = jnp.broadcast_to(levels[:, ny + y : ny + y + 1], (deep, lanes))
            coef_ref[plane, y] = jnp.where(first_lanes, front, rear)

    for step in range(DEGREE - 2):
        filter_step(0, step)
    send_halos(1, 0)
    filter_step(0, DEGREE - 2)
    filter_step(1, 0)
    filter_step(0, DEGREE - 1)
    for step in range(1, DEGREE):
        filter_step(1, step)

    def unpacked(one, two):
        shape = (share * rows, deep, lanes)
        one, two = one.reshape(shape), two.reshape(shape)
        lower = lax.broadcasted_iota(jnp.int32, shape, 2) < turn
        whole = jnp.concatenate(
            [jnp.where(lower, one, turned(two)), jnp.where(lower, turned(one), two)], axis=1
        )
        return split(whole.reshape(cells, lanes))

    part[...] = jnp.zeros_like(part)
    cross[...] = jnp.zeros_like(cross)

    @pl.loop(0, CHUNKS)
    def _(chunk):
        at = pl.ds(pl.multiple_of(chunk * cells, cells), cells)
        for half in range(2):
            for offset in range(1, n_orb):
                outward(half, chunk, offset).wait_recv()
            outward_own(half, chunk).wait()
        for block in range(n_orb):
            columns = pl.ds(block * lanes, lanes)
            high[at, columns], low[at, columns] = unpacked(
                mixed[0, chunk, :, :, :, columns], mixed[1, chunk, :, :, :, columns]
            )
        head, tail = high[at], low[at]
        part[...] += transposed_dot(head, head)
        cross[...] += transposed_dot(head, tail)

    part[...] = (part[...] + 2.0 * cross[...]) * (1.0 / (CHUNKS * cells * n_space * n_orb))

    def pair_peer(offset):
        return lax.rem(pair + offset, n_pair)

    def send_half():
        return remote(
            part.at[core_rows(1 - core)], landed_half, half_send, half_recv, 2 * pair + 1 - core, me_o
        )

    def send_rows(offset):
        peer = pair_peer(offset)
        return remote(
            part.at[row_block(peer)], landed.at[offset - 1],
            rows_send.at[offset], rows_recv.at[offset], 2 * peer + core, me_o,
        )

    def send_cols(offset):
        peer = orb_peer(offset)
        return remote(
            summed.at[:, lane_block(peer)], landed_cols.at[offset - 1],
            cols_send.at[offset], cols_recv.at[offset], me_s, peer,
        )

    def gather_cols(offset):
        block = total.at[row_block(pair), lane_block(me_o)]
        return remote(block, block, gcols_send.at[offset], gcols_recv.at[offset], me_s, orb_peer(offset))

    def gather_rows(offset):
        block = total.at[row_block(pair)]
        return remote(
            block, block, grows_send.at[offset], grows_recv.at[offset], 2 * pair_peer(offset) + core, me_o
        )

    def gather_half():
        block = total.at[core_rows(core)]
        return remote(block, block, ghalf_send, ghalf_recv, 2 * pair + 1 - core, me_o)

    send_half().start()
    send_half().wait_recv()
    part[core_rows(core)] += landed_half[...]
    for offset in range(1, n_pair):
        send_rows(offset).start()
    value = part[row_block(pair)]
    for offset in range(1, n_pair):
        send_rows(offset).wait_recv()
        value = value + landed[offset - 1]
    summed[...] = value
    for offset in range(1, n_orb):
        send_cols(offset).start()
    value = summed[:, lane_block(me_o)]
    for offset in range(1, n_orb):
        send_cols(offset).wait_recv()
        value = value + landed_cols[offset - 1]
    total[row_block(pair), lane_block(me_o)] = value
    for offset in range(1, n_orb):
        gather_cols(offset).start()
    for offset in range(1, n_orb):
        gather_cols(offset).wait_recv()
    for offset in range(1, n_pair):
        gather_rows(offset).start()
    for chunk in range(GATHERED):
        for half in range(2):
            gather_start(half, chunk)
    for offset in range(1, n_pair):
        gather_rows(offset).wait_recv()
    gather_half().start()
    gather_half().wait_recv()

    one_sided = total[...]
    intersection = 0.5 * (one_sided + one_sided.T)
    squares = jnp.sum(intersection * intersection, axis=0, keepdims=True)
    norm_scale = jnp.sqrt(jnp.sum(squares, axis=1, keepdims=True) + 1e-06)
    on_diagonal = lax.broadcasted_iota(jnp.int32, (norb, norb), 0) == lax.broadcasted_iota(
        jnp.int32, (norb, norb), 1
    )

    def factor_of(term):
        return jnp.where(on_diagonal, 1.5, 0.0) - 0.5 * term

    scaled = intersection / norm_scale
    inverse = factor_of(scaled)
    z_ref[...] = inverse
    y_ref[...] = product(split(scaled), split(inverse))

    @pl.loop(1, NS_ITERS - 1)
    def _(step):
        ys, zs = split(y_ref[...]), split(z_ref[...])
        fs = split(factor_of(product(zs, ys)))
        y_ref[...] = product(ys, fs)
        z_ref[...] = product(fs, zs)

    ys, zs = split(y_ref[...]), split(z_ref[...])
    fs = split(factor_of(product(zs, ys)))
    z_ref[...] = product(fs, zs) / jnp.sqrt(norm_scale)

    @pl.loop(GATHERED, CHUNKS)
    def _(chunk):
        at = pl.ds(pl.multiple_of(chunk * cells, cells), cells)
        value = product((high[at], low[at]), split(z_ref[...]))
        white[chunk - GATHERED] = value.reshape(share, rows, nz, norb)
        for offset in range(1, n_orb):
            back(chunk, offset).start()
        back_own_copy(chunk).start()

    own = split(z_ref[:, lane_block(me_o)])

    for chunk in range(GATHERED):
        at = pl.ds(chunk * cells, cells)
        ys = pl.ds(chunk * rows, rows)
        value = product((high[at], low[at]), own)
        out_ref[pl.ds(me_o * share, share), ys] = value.reshape(share, rows, nz, lanes)
        for turn_at in range(1, n_orb):
            owned = pl.ds(lax.rem(me_o + turn_at, n_orb) * share, share)
            for half in range(2):
                for offset in range(1, n_orb):
                    gather(half, chunk, offset, turn_at).wait_recv()
                extra[half, chunk, turn_at, :, :, :, lane_block(me_o)] = last[half, owned, ys]
            parts = []
            for block in range(n_orb):
                columns = pl.ds(block * lanes, lanes)
                parts.append(
                    unpacked(
                        extra[0, chunk, turn_at, :, :, :, columns],
                        extra[1, chunk, turn_at, :, :, :, columns],
                    )
                )
            field = tuple(jnp.concatenate([p[i] for p in parts], axis=1) for i in range(2))
            out_ref[owned, ys] = product(field, own).reshape(share, rows, nz, lanes)

    send_half().wait_send()
    gather_half().wait_send()
    for offset in range(1, n_pair):
        send_rows(offset).wait_send()
        gather_rows(offset).wait_send()
    for offset in range(1, n_orb):
        send_cols(offset).wait_send()
        gather_cols(offset).wait_send()
    for half in range(2):
        for step in range(DEGREE):

            @pl.loop(0, CHUNKS)
            def _(chunk):
                halo(half, step, chunk, 0).wait_send()
                halo(half, step, chunk, 1).wait_send()

    @pl.loop(0, CHUNKS)
    def _(chunk):
        for offset in range(1, n_orb):
            outward(0, chunk, offset).wait_send()
            outward(1, chunk, offset).wait_send()

    for chunk in range(GATHERED):
        for half in range(2):
            for turn_at in range(1, n_orb):
                for offset in range(1, n_orb):
                    gather(half, chunk, offset, turn_at).wait_send()

    @pl.loop(GATHERED, CHUNKS)
    def _(chunk):
        back_own_copy(chunk).wait()
        for offset in range(1, n_orb):
            back(chunk, offset).wait()


def body(n_space, n_orb, orbitals, potential):
    planes, ny, nz, lanes = orbitals.shape
    norb = lanes * n_orb
    piece = norb // n_space
    block = (CHUNKS, planes // n_orb, ny // CHUNKS, nz, norb)
    cells = planes * ny * nz // n_orb
    by_depth = jnp.transpose(potential.reshape(planes, ny, 2, nz // 2), (0, 3, 2, 1))
    by_depth = by_depth.reshape(planes, nz // 2, 2 * ny)
    f32 = jnp.float32
    dma = pltpu.SemaphoreType.DMA
    return pl.pallas_call(
        functools.partial(kernel, n_space, n_orb),
        out_shape=jax.ShapeDtypeStruct(orbitals.shape, f32),
        in_specs=[pl.BlockSpec(memory_space=pl.ANY), pl.BlockSpec(memory_space=pltpu.VMEM)],
        out_specs=pl.BlockSpec(memory_space=pltpu.VMEM),
        scratch_shapes=[
            pltpu.VMEM((planes, ny, nz, lanes), f32),
            pltpu.VMEM((planes, ny, nz // 2, lanes), f32),
            pltpu.VMEM((2, DEGREE, planes + 2 * REACH, ny, nz // 2, lanes), f32),
            pltpu.VMEM((2, planes, ny, nz // 2, lanes), f32),
            pltpu.VMEM((2,) + block[:3] + (nz // 2, norb), f32),
            pltpu.VMEM((2, GATHERED, n_orb) + block[1:3] + (nz // 2, norb), f32),
            pltpu.VMEM((cells, norb), jnp.bfloat16),
            pltpu.VMEM((cells, norb), jnp.bfloat16),
            pltpu.VMEM((norb, norb), f32),
            pltpu.VMEM((norb, norb), f32),
            pltpu.VMEM((norb // 2, norb), f32),
            pltpu.VMEM((n_space // 2 - 1, piece, norb), f32),
            pltpu.VMEM((piece, norb), f32),
            pltpu.VMEM((n_orb - 1, piece, lanes), f32),
            pltpu.VMEM((norb, norb), f32),
            pltpu.VMEM((norb, norb), f32),
            pltpu.VMEM((norb, norb), f32),
            pltpu.VMEM((CHUNKS - GATHERED,) + block[1:], f32),
            dma,
            dma((2, DEGREE, CHUNKS, 2)),
            dma((2, DEGREE, CHUNKS, 2)),
            dma((2, CHUNKS, n_orb)),
            dma((2, CHUNKS, n_orb)),
            dma((2, CHUNKS)),
            dma((2, GATHERED, n_orb, n_orb)),
            dma((2, GATHERED, n_orb, n_orb)),
            dma,
            dma,
            dma,
            dma,
            dma((n_space // 2,)),
            dma((n_space // 2,)),
            dma((n_orb,)),
            dma((n_orb,)),
            dma((n_orb,)),
            dma((n_orb,)),
            dma((n_space // 2,)),
            dma((n_space // 2,)),
            dma((CHUNKS, n_orb)),
            dma((CHUNKS, n_orb)),
            dma((CHUNKS,)),
        ],
        compiler_params=pltpu.CompilerParams(
            collective_id=0, has_side_effects=True, vmem_limit_bytes=60 * 1024 * 1024
        ),
        cost_estimate=pl.CostEstimate(
            flops=20_000_000_000, bytes_accessed=8_000_000, transcendentals=0
        ),
    )(orbitals, by_depth)


def solution(mesh):
    return jax.shard_map(
        functools.partial(body, mesh.shape["space"], mesh.shape["orb"]),
        mesh=mesh,
        in_specs=(P("space", None, None, "orb"), P("space", None, None)),
        out_specs=P("space", None, None, "orb"),
        check_vma=False,
    )
```
